32 devices in a mesh: patch: 4 (over x, core), proto: 8 (over z, y).
Axes of the slice: x: 2, y: 2, z: 4, core: 2. Of those that a mesh axis runs over, the one named last changes fastest.
Arguments:
- student_feats: bfloat16 [8192, 256], P(('patch', 'proto')), may hold values from -50 to 50
- teacher_feats: bfloat16 [8192, 256], P(('patch', 'proto')), may hold values from -50 to 50
- proto_weight: bfloat16 [256, 131072], P(None, 'proto'), may hold values from -4 to 4
- mask_index: int32 [1024], P(('patch', 'proto')), may hold values from 0 to 255, as said below
- row_weight: bfloat16 [1024], P(('patch', 'proto')), may hold values from 0.5 to 4
Outputs:
- grad_student: float32 [1024, 256], P(('patch', 'proto'))
- grad_proto: float32 [256, 131072], P('patch', 'proto')
- loss: float32 [], replicated
The draws below stay inside these ranges and needn't reach their ends.
Inputs may be any that keep to these rules, and one draw needn't show every extreme that they name: `mask_index`: entries k * 32 to (k + 1) * 32 - 1 are distinct patch positions of image k, counted from that image's first patch.
All inputs are finite; a program needn't handle non-finite values.
Results may differ from the reference program's by a relative error of at most 0.0057.
Values may be sent and summed in bfloat16 or wider, within the bound.
A program may use at most 128 MiB of HBM per device.

```python
import math
import jax
import jax.numpy as jnp
from jax import lax

D = 256
P_SIZE = 131072
PATCH_DEV = 256
MASK_DEV = 32
SK_ITERS = 3
PATCHES = 8192
MASKED = 1024


regions = 16


def base_normal(key):
    return jnp.clip(jax.random.normal(jax.random.fold_in(key, 11), (D, P_SIZE), jnp.float32), -5.0, 5.0)


def anchor_table(key):
    return jnp.clip(jax.random.normal(jax.random.fold_in(key, 13), (D, regions), jnp.float32), -5.0, 5.0)


def proto_region(key):
    first = jax.random.randint(jax.random.fold_in(key, 14), (P_SIZE,), 0, regions)
    second = jax.random.randint(jax.random.fold_in(key, 15), (P_SIZE,), 0, regions)
    return jnp.minimum(first, second).astype(jnp.int32)


def row_region(key):
    return jax.random.randint(jax.random.fold_in(key, 21), (PATCHES,), 0, regions).astype(jnp.int32)


def draw_proto_weight(key, part):
    base = base_normal(key)
    anchors = anchor_table(key)
    pulled = base + jnp.take(anchors, proto_region(key), axis=1)
    spread = 0.7
    scale = jnp.exp(jax.random.uniform(jax.random.fold_in(key, 12), (P_SIZE,), jnp.float32, -spread, spread))
    values = jnp.clip(pulled * scale[None, :] / math.sqrt(D), -4.0, 4.0)
    return values.astype(jnp.bfloat16)


def feature_rows(key, salt, amp_low, amp_high, ramp_low, ramp_high):
    anchors = anchor_table(key)
    centers = jnp.take(anchors, row_region(key), axis=1).T / math.sqrt(D)
    amplitude = jax.random.uniform(jax.random.fold_in(key, salt), (PATCHES, 1), jnp.float32, amp_low, amp_high)
    along = jnp.arange(PATCHES, dtype=jnp.float32)[:, None] / float(PATCHES - 1)
    amplitude = amplitude * (ramp_low + (ramp_high - ramp_low) * along)
    noise = jnp.clip(jax.random.normal(jax.random.fold_in(key, salt + 1), (PATCHES, D), jnp.float32), -5.0, 5.0)
    row_scale = jnp.exp(jax.random.uniform(jax.random.fold_in(key, salt + 2), (PATCHES, 1), jnp.float32, 0.0, math.log(10.0)))
    rows = (amplitude * centers + noise / math.sqrt(D)) * row_scale
    return jnp.clip(rows, -50.0, 50.0)


def draw_student_feats(key, part):
    rows = feature_rows(key, 31, 0.5, 2.0, 1.0, 6.0)
    return rows.astype(jnp.bfloat16)


def draw_teacher_feats(key, part):
    rows = feature_rows(key, 41, 1.0, 3.0, 1.0, 1.0)
    return rows.astype(jnp.bfloat16)


def draw_mask_index(key, part):
    subkeys = jax.random.split(jax.random.fold_in(key, 51), MASKED // MASK_DEV)
    picks = jax.vmap(lambda subkey: jax.random.permutation(subkey, PATCH_DEV)[:MASK_DEV])(subkeys)
    return picks.reshape(-1).astype(jnp.int32)


def block_scale(stream_key, dims, cuts, smallest, high):
    gain = 1.0
    for dim, parts in cuts:
        draws = jax.random.uniform(jax.random.fold_in(jax.random.fold_in(stream_key, 6), dim), (parts,), jnp.float32, smallest / len(cuts), high / len(cuts))
        gain = gain * jnp.repeat(jnp.exp(draws), dims[dim] // parts).reshape((-1,) + (1,) * (len(dims) - 1 - dim))
    return gain


def setup_inputs(seed: int = 0) -> dict:
    key_list = jax.random.split(jax.random.key(seed), 6)
    student_feats = draw_student_feats(jax.random.fold_in(key_list[5], 71), 0)
    teacher_feats = draw_teacher_feats(jax.random.fold_in(key_list[5], 71), 0)
    proto_weight = draw_proto_weight(jax.random.fold_in(key_list[5], 71), 0)
    mask_index = draw_mask_index(jax.random.fold_in(key_list[5], 71), 0)
    row_weight = jnp.clip(jnp.exp(math.log(4.0) - 2.0794415 * jax.random.uniform(key_list[4], (MASKED,), jnp.float32) ** block_scale(key_list[4], (MASKED,), ((0, 32),), -0.2, 0.2)), 0.5, 4.0).astype(jnp.bfloat16)
    return dict(student_feats=student_feats, teacher_feats=teacher_feats, proto_weight=proto_weight, mask_index=mask_index, row_weight=row_weight)


eps = 1e-06
teacher_temp = 0.07
student_temp = 0.1

def unit_rows(values):
    values = values.astype(jnp.float32)
    inverse = lax.rsqrt(lax.optimization_barrier(jnp.sum(values * values, axis=1)) + eps)
    return (values * inverse[:, None], inverse)

def reference(student_feats, teacher_feats, proto_weight, mask_index, row_weight):
    images = jnp.arange(MASKED, dtype=jnp.int32) // MASK_DEV
    position = (mask_index.astype(jnp.int32) + images * PATCH_DEV).astype(jnp.int32)
    unit_student, inverse_student = unit_rows(jnp.take(student_feats, position, axis=0))
    unit_teacher, _ = unit_rows(jnp.take(teacher_feats, position, axis=0))
    student_rows = unit_student.astype(jnp.bfloat16)
    teacher_rows = unit_teacher.astype(jnp.bfloat16)
    weights = row_weight.astype(jnp.float32)
    w_float = proto_weight.astype(jnp.float32)
    col_inverse = lax.rsqrt(lax.optimization_barrier(jnp.sum(w_float * w_float, axis=0)) + eps)
    unit_proto = w_float * col_inverse[None, :]
    proto_unit = unit_proto.astype(jnp.bfloat16)
    block = min(P_SIZE, 4096)
    block_count = P_SIZE // block

    def blocks(array):
        return jnp.transpose(array.reshape(array.shape[0], block_count, block), (1, 0, 2))
    proto_blocks = blocks(proto_unit)
    unit_blocks = blocks(unit_proto)
    inverse_blocks = col_inverse.reshape(block_count, block)
    highest = lax.Precision.HIGHEST

    def teacher_exp(proto_block):
        return jnp.exp(jnp.dot(teacher_rows, proto_block, preferred_element_type=jnp.float32) / teacher_temp)
    scale_rows = jnp.ones((MASKED,), jnp.float32)
    col_blocks = None
    for sweep in range(SK_ITERS):

        def sweep_block(row_partial, proto_block):
            table = teacher_exp(proto_block)
            scale_cols = 1.0 / jnp.dot(scale_rows, table, precision=highest)
            return (row_partial + jnp.dot(table, scale_cols, precision=highest), scale_cols)
        row_total, col_blocks = lax.scan(sweep_block, jnp.zeros((MASKED,), jnp.float32), proto_blocks)
        scale_rows = 1.0 / row_total

    def exp_block(exp_partial, proto_block):
        logits = jnp.dot(student_rows, proto_block, preferred_element_type=jnp.float32) / student_temp
        return (exp_partial + lax.optimization_barrier(jnp.sum(jnp.exp(logits), axis=1)), None)
    exp_total, _ = lax.scan(exp_block, jnp.zeros((MASKED,), jnp.float32), proto_blocks)
    log_total = jnp.log(exp_total)

    def final_block(carry, pieces):
        feature_partial, loss_partial = carry
        proto_block, unit_block, inverse_block, scale_cols = pieces
        codes = teacher_exp(proto_block) * scale_rows[:, None] * scale_cols[None, :]
        logits = jnp.dot(student_rows, proto_block, preferred_element_type=jnp.float32) / student_temp
        student_probs = jnp.exp(logits) / exp_total[:, None]
        grad_logits = (weights[:, None] * (student_probs - codes)).astype(jnp.bfloat16)
        loss_partial = loss_partial + jnp.sum(weights[:, None] * codes * (log_total[:, None] - logits))
        feature_partial = feature_partial + jnp.dot(grad_logits, proto_block.T, preferred_element_type=jnp.float32) / student_temp
        head = jnp.dot(student_rows.T, grad_logits, preferred_element_type=jnp.float32) / student_temp
        inner = lax.optimization_barrier(jnp.sum(unit_block * head, axis=0))
        return ((feature_partial, loss_partial), inverse_block[None, :] * (head - unit_block * inner[None, :]))
    start_carry = (jnp.zeros((MASKED, D), jnp.float32), jnp.zeros((), jnp.float32))
    (feature_grad, loss_sum), grad_blocks = lax.scan(final_block, start_carry, (proto_blocks, unit_blocks, inverse_blocks, col_blocks))
    grad_proto = jnp.transpose(grad_blocks, (1, 0, 2)).reshape(D, P_SIZE)
    grad_student = inverse_student[:, None] * (feature_grad - unit_student * lax.optimization_barrier(jnp.sum(unit_student * feature_grad, axis=1))[:, None])
    loss = loss_sum / jnp.sum(weights)
    return (grad_student, grad_proto, loss)
```

```python
import functools

import jax
import jax.numpy as jnp
from jax import lax
from jax.experimental import pallas as pl
from jax.experimental.pallas import tpu as pltpu
from jax.sharding import PartitionSpec as P

SK_ITERS = 3

eps = 1e-06
teacher_temp = 0.07
student_temp = 0.1
AXES = ("patch", "proto")
LANES = 128


def unit_rows(values):
    values = values.astype(jnp.float32)
    inverse = lax.rsqrt(jnp.sum(values * values, axis=1) + eps)
    return (values * inverse[:, None], inverse)


def unit_block(w_ref):
    w = w_ref[...].astype(jnp.float32)
    inverse = lax.rsqrt(jnp.sum(w * w, axis=0, keepdims=True) + eps)
    unit = w * inverse
    return unit, inverse, unit.astype(jnp.bfloat16)


def scaled_dot(rows_ref, block, temp):
    return jnp.dot(rows_ref[...], block, preferred_element_type=jnp.float32) * (1.0 / temp)


def lane_sums(values):
    total = values[:, :LANES]
    for start in range(LANES, values.shape[1], LANES):
        total = total + values[:, start : start + LANES]
    return total


def sweep_kernel(first, last, t_ref, s_ref, w_ref, r_ref, row_ref, extra_ref, c_ref, row_acc, extra_acc):
    step = pl.program_id(0)

    @pl.when(step == 0)
    def _():
        row_acc[...] = jnp.zeros_like(row_acc)
        extra_acc[...] = jnp.zeros_like(extra_acc)

    _, _, block = unit_block(w_ref)
    table = jnp.exp(scaled_dot(t_ref, block, teacher_temp))
    weighted = table if first else table * r_ref[...]
    cols = 1.0 / jnp.sum(weighted, axis=0, keepdims=True)
    c_ref[...] = cols
    part = table * cols
    row_acc[...] += lane_sums(part)
    if first:
        extra_acc[...] += lane_sums(jnp.exp(scaled_dot(s_ref, block, student_temp)))
    if last:
        extra_acc[...] += lane_sums(part * scaled_dot(s_ref, block, student_temp))

    @pl.when(step == pl.num_programs(0) - 1)
    def _():
        row_ref[...] = jnp.sum(row_acc[...], axis=1, keepdims=True)
        extra_ref[...] = jnp.sum(extra_acc[...], axis=1, keepdims=True)


def final_kernel(t_ref, s_ref, st_ref, w_ref, wr_ref, wt_ref, c_ref, feat_ref, grad_ref):
    step = pl.program_id(0)

    @pl.when(step == 0)
    def _():
        feat_ref[...] = jnp.zeros_like(feat_ref)

    unit, inverse, block = unit_block(w_ref)
    codes = jnp.exp(scaled_dot(t_ref, block, teacher_temp)) * c_ref[...] * wr_ref[...]
    probs = jnp.exp(scaled_dot(s_ref, block, student_temp)) * wt_ref[...]
    grad = (probs - codes).astype(jnp.bfloat16)
    feat_ref[...] += lax.dot_general(
        grad, block, (((1,), (1,)), ((), ())), preferred_element_type=jnp.float32
    )
    head = scaled_dot(st_ref, grad, student_temp)
    inner = jnp.sum(unit * head, axis=0, keepdims=True)
    grad_ref[...] = (inverse * (head - unit * inner)).astype(jnp.bfloat16)


def whole(shape):
    return pl.BlockSpec(shape, lambda i: (0, 0))


def split(rows, width):
    return pl.BlockSpec((rows, width), lambda i: (0, i))


def params():
    return pltpu.CompilerParams(
        dimension_semantics=("arbitrary",), vmem_limit_bytes=50 * 1024 * 1024
    )


def block_width(rows, cols):
    return min(cols, max(LANES, 262144 // rows))


def sweep(first, last, teacher, student, w_own, scale_rows):
    rows, depth = teacher.shape
    cols = w_own.shape[1]
    width = block_width(rows, cols)
    return pl.pallas_call(
        functools.partial(sweep_kernel, first, last),
        grid=(cols // width,),
        in_specs=[whole((rows, depth)), whole((rows, depth)), split(depth, width), whole((rows, 1))],
        out_specs=[whole((rows, 1)), whole((rows, 1)), split(1, width)],
        out_shape=[
            jax.ShapeDtypeStruct((rows, 1), jnp.float32),
            jax.ShapeDtypeStruct((rows, 1), jnp.float32),
            jax.ShapeDtypeStruct((1, cols), jnp.float32),
        ],
        scratch_shapes=[pltpu.VMEM((rows, LANES), jnp.float32)] * 2,
        compiler_params=params(),
    )(teacher, student, w_own, scale_rows)


def gradients(teacher, student, w_own, weight_rows, weight_total, scale_cols):
    rows, depth = teacher.shape
    cols = w_own.shape[1]
    width = block_width(rows, cols)
    return pl.pallas_call(
        final_kernel,
        grid=(cols // width,),
        in_specs=[
            whole((rows, depth)),
            whole((rows, depth)),
            whole((depth, rows)),
            split(depth, width),
            whole((rows, 1)),
            whole((rows, 1)),
            split(1, width),
        ],
        out_specs=[whole((rows, depth)), split(depth, width)],
        out_shape=[
            jax.ShapeDtypeStruct((rows, depth), jnp.float32),
            jax.ShapeDtypeStruct((depth, cols), jnp.bfloat16),
        ],
        compiler_params=params(),
    )(teacher, student, student.T, w_own, weight_rows, weight_total, scale_cols)


def on_device(student_feats, teacher_feats, proto_weight, mask_index, row_weight):
    unit_student, inverse_student = unit_rows(jnp.take(student_feats, mask_index, axis=0))
    unit_teacher, _ = unit_rows(jnp.take(teacher_feats, mask_index, axis=0))
    depth = unit_student.shape[1]
    own = jnp.concatenate(
        [
            unit_student.astype(jnp.bfloat16),
            unit_teacher.astype(jnp.bfloat16),
            jnp.broadcast_to(row_weight[:, None], (row_weight.shape[0], LANES)),
        ],
        axis=1,
    )
    rows = lax.all_gather(own, AXES, axis=0, tiled=True)
    student, teacher = rows[:, :depth], rows[:, depth : 2 * depth]
    weights = rows[:, 2 * depth : 2 * depth + 1].astype(jnp.float32)
    share = proto_weight.shape[1] // lax.axis_size("patch")
    w_own = lax.dynamic_slice_in_dim(proto_weight, lax.axis_index("patch") * share, share, 1)

    scale_rows = jnp.ones((student.shape[0], 1), jnp.float32)
    for step in range(SK_ITERS):
        first, last = step == 0, step == SK_ITERS - 1
        row_part, extra, scale_cols = sweep(first, last, teacher, student, w_own, scale_rows)
        if first or last:
            both = lax.psum(jnp.concatenate([row_part[:, 0], extra[:, 0]]), AXES)
            row_total, extra = both[: row_part.shape[0], None], both[row_part.shape[0] :, None]
        else:
            row_total = lax.psum(row_part[:, 0], AXES)[:, None]
        scale_rows = 1.0 / row_total
        if first:
            exp_total = extra
    loss = jnp.sum(weights * (jnp.log(exp_total) - scale_rows * extra)) / jnp.sum(weights)

    feature, grad_own = gradients(
        teacher, student, w_own, weights * scale_rows, weights / exp_total, scale_cols
    )
    grad_proto = lax.all_to_all(grad_own, "patch", split_axis=0, concat_axis=1, tiled=True)
    feature_grad = lax.psum_scatter(feature, AXES, scatter_dimension=0, tiled=True) / student_temp
    grad_student = inverse_student[:, None] * (
        feature_grad - unit_student * jnp.sum(unit_student * feature_grad, axis=1)[:, None]
    )
    return (grad_student, grad_proto.astype(jnp.float32), loss)


def solution(mesh):
    in_specs = (P(AXES, None), P(AXES, None), P(None, "proto"), P(AXES), P(AXES))
    out_specs = (P(AXES, None), P("patch", "proto"), P())
    return jax.shard_map(
        on_device, mesh=mesh, in_specs=in_specs, out_specs=out_specs, check_vma=False
    )
```
